32 devices in a mesh: row: 4 (over y, core), col: 8 (over z, x).
Axes of the slice: x: 2, y: 2, z: 4, core: 2. Of those that a mesh axis runs over, the one named last changes fastest.
Arguments:
- kernel: float32 [4, 4, 256, 2, 8, 256], P(None, 'row', None, None, 'col'), as said below
- targets: float32 [4, 4, 256, 512], P(None, 'row', None, 'col'), may hold values from -6 to 6
Outputs:
- factored: float32 [4, 4, 256, 2, 8, 256], P(None, 'row', None, None, 'col')
- solved_targets: float32 [4, 4, 256, 512], P(None, 'row', None, 'col')
The draws below stay inside these ranges and needn't reach their ends.
Inputs may be any that keep to these rules, and one draw needn't show every extreme that they name: kernel is symmetric positive definite with eigenvalues between about 0.5 and 38.
All inputs are finite; a program needn't handle non-finite values.
Results may differ from the reference program's by a relative error of at most 0.0001.
Values sent between devices are 32-bit elements; how exact they have to be, the bound alone decides.
A program may use at most 64 MiB of HBM per device.

```python
import jax
import jax.numpy as jnp
from jax import lax

NB = 256
CB_DEV = 2
TARGETS = 512
RB_DEV = 4
ORDER = 4096
N_ROW = 4
N_COL = 8


def draw_kernel(key, part):
    feature_key = jax.random.fold_in(key, 11)
    noise_key = jax.random.fold_in(key, 23)
    features = 2 * NB
    loadings = jax.random.normal(feature_key, (ORDER, features), jnp.float32) / jnp.sqrt(1.0 * features)
    noise = jax.random.uniform(noise_key, (ORDER,), jnp.float32, 0.5, 1.5)
    matrix = jnp.dot(loadings, loadings.T, precision=lax.Precision.HIGHEST, preferred_element_type=jnp.float32)
    matrix = 0.5 * (matrix + matrix.T)
    places = jnp.arange(ORDER)
    matrix = matrix.at[places, places].add(noise)
    return matrix.reshape(RB_DEV, N_ROW, NB, CB_DEV, N_COL, NB)


def block_scale(own_key, shape, pieces, smallest, largest):
    gain, own = 1.0, jax.random.fold_in(own_key, 6)
    for position, parts in pieces:
        heights = jnp.exp(jax.random.uniform(jax.random.fold_in(own, position), (parts,), jnp.float32, smallest / len(pieces), largest / len(pieces)))
        gain = gain * jnp.repeat(heights, shape[position] // parts).reshape([-1 if axis == position else 1 for axis in range(len(shape))])
    return gain


def bell_draw(rng, dims, spread, most, pieces=(), held_as=jnp.bfloat16):
    array = spread * jax.random.normal(rng, dims, jnp.float32)
    if pieces:
        array = array * block_scale(rng, dims, pieces, -0.22, 0.18)
    return jnp.clip(array, -most, most).astype(held_as)


def setup_inputs(seed: int = 0) -> dict:
    arg_keys = jax.random.split(jax.random.key(seed), 3)
    kernel = draw_kernel(jax.random.fold_in(arg_keys[2], 71), 0)
    targets = bell_draw(arg_keys[1], (RB_DEV, N_ROW, NB, TARGETS), 1.0, 6.0, ((1, 4), (3, 8)), jnp.float32)
    return {"kernel": kernel, "targets": targets}


def reference(kernel, targets):
    matrix = kernel.reshape(ORDER, ORDER)
    right_sides = targets.reshape(ORDER, TARGETS)
    for section in range(2):
        offset = section * NB
        corner = matrix[offset:offset + NB, offset:offset + NB]
        lower_factor = jnp.linalg.cholesky(corner)
        beneath = matrix[offset + NB:, offset:offset + NB]
        panel = jax.scipy.linalg.solve_triangular(lower_factor, beneath.T, lower=True).T
        product = jnp.dot(panel.astype(jnp.float32), panel.T.astype(jnp.float32), precision=lax.Precision.HIGHEST, preferred_element_type=jnp.float32)
        matrix = matrix.at[offset + NB:, offset + NB:].add(-product)
        column = jnp.concatenate([jnp.zeros((offset, NB), jnp.float32), lower_factor, panel], axis=0)
        matrix = matrix.at[:, offset:offset + NB].set(column)
        solved = jax.scipy.linalg.solve_triangular(lower_factor, right_sides[offset:offset + NB], lower=True)
        update = jnp.dot(panel.astype(jnp.float32), solved.astype(jnp.float32), precision=lax.Precision.HIGHEST, preferred_element_type=jnp.float32)
        right_sides = right_sides.at[offset + NB:].add(-update)
        right_sides = right_sides.at[offset:offset + NB].set(solved)
    return (matrix.reshape(kernel.shape), right_sides.reshape(targets.shape))
```

```python
import functools

import jax
import jax.numpy as jnp
from jax import lax
from jax.experimental import pallas as pl
from jax.experimental.pallas import tpu as pltpu
from jax.sharding import PartitionSpec as P

STEP = 8
BASE = 128


def exact_dot(a, b, dims):
    return lax.dot_general(
        a, b, (dims, ((), ())), precision=lax.Precision.HIGHEST, preferred_element_type=jnp.float32
    )


def halves(a):
    high = a.astype(jnp.bfloat16)
    low = (a - high.astype(jnp.float32)).astype(jnp.bfloat16)
    return high, low


def split_dot(a, b, dims):
    def dot(x, y):
        return lax.dot_general(x, y, (dims, ((), ())), preferred_element_type=jnp.float32)

    a_high, a_low = a
    b_high, b_low = b
    return dot(a_high, b_high) + (dot(a_high, b_low) + dot(a_low, b_high))


def base_inverse(block):
    groups = BASE // STEP
    rows = lax.broadcasted_iota(jnp.int32, (STEP, BASE), 0)
    lanes = lax.broadcasted_iota(jnp.int32, (STEP, BASE), 1)
    full = (STEP, BASE)
    main = [block[STEP * p : STEP * (p + 1), :] for p in range(groups)]
    side = [(lanes == rows + STEP * p).astype(jnp.float32) for p in range(groups)]
    done = []
    for q in range(groups):
        here = main[q]
        first = STEP * q
        columns = [jnp.broadcast_to(here[:, first + j : first + j + 1], full) for j in range(STEP)]
        spot = [
            [jnp.broadcast_to(columns[j][i : i + 1, :], full) if i <= j else None for j in range(STEP)]
            for i in range(STEP)
        ]
        mains = [jnp.broadcast_to(here[i : i + 1, :], full) for i in range(STEP)]
        sides = [jnp.broadcast_to(side[q][i : i + 1, :], full) for i in range(STEP)]
        ratio = [[None] * STEP for _ in range(STEP)]
        recips = []
        for k in range(STEP):
            recip = 1.0 / spot[k][k]
            recips.append(recip)
            for i in range(k + 1, STEP):
                ratio[k][i] = spot[k][i] * recip
            for i in range(k + 1, STEP):
                for j in range(i, STEP):
                    spot[i][j] = spot[i][j] - ratio[k][i] * spot[k][j]
                mains[i] = mains[i] - ratio[k][i] * mains[k]
                sides[i] = sides[i] - ratio[k][i] * sides[k]
        scaled = jnp.zeros(full, jnp.float32)
        for k in range(STEP):
            scaled = jnp.where(rows == k, sides[k] * lax.rsqrt(spot[k][k]), scaled)
        done.append(scaled)
        if q == groups - 1:
            break
        mains = [mains[k] * recips[k] for k in range(STEP)]
        sides = [sides[k] * recips[k] for k in range(STEP)]
        for k in range(STEP - 1, 0, -1):
            for i in range(k):
                mains[i] = mains[i] - ratio[i][k] * mains[k]
                sides[i] = sides[i] - ratio[i][k] * sides[k]
        for p in range(q + 1, groups):
            factor = [
                jnp.broadcast_to(main[p][:, first + k : first + k + 1], full) for k in range(STEP)
            ]
            for target, source in ((main, mains), (side, sides)):
                terms = [factor[k] * source[k] for k in range(STEP)]
                while len(terms) > 1:
                    terms = [terms[t] + terms[t + 1] for t in range(0, len(terms), 2)]
                target[p] = target[p] - terms[0]
    return jnp.concatenate(done, axis=0)


def compute_kernel(
    nb, corner_ref, cols_ref, rhs_ref, rows_ref, own_ref, own_rhs_ref, out_ref, out_rhs_ref,
    work, cols, inverse_ref, panel,
):
    size = corner_ref.shape[0]
    steps = size // BASE
    width = cols_ref.shape[1]
    row_blocks = rows_ref.shape[0] // nb
    row_count = lax.axis_size("row")
    row_place = lax.axis_index("row")
    col_place = lax.axis_index("col")
    work[...] = corner_ref[...]
    cols[:, :width] = cols_ref[...]
    cols[:, width:] = rhs_ref[...]
    for b in range(steps):
        at = slice(b * BASE, (b + 1) * BASE)
        inverse = base_inverse(work[at, at])
        inverse_ref[at, :] = inverse
        cols[at, :] = exact_dot(inverse, cols[at, :], ((1,), (0,)))
        if b == steps - 1:
            break
        rest = slice((b + 1) * BASE, size)
        upper = exact_dot(inverse, work[at, rest], ((1,), (0,)))
        work[at, rest] = upper
        work[rest, rest] = work[rest, rest] - exact_dot(upper, upper, ((0,), (0,)))
        cols[rest, :] = cols[rest, :] - exact_dot(upper, cols[at, :], ((0,), (0,)))
    solved = halves(cols[...])
    row_in = lax.broadcasted_iota(jnp.int32, (nb, nb), 0)
    col_in = lax.broadcasted_iota(jnp.int32, (nb, nb), 1)
    for rb in range(row_blocks):
        block_row = rb * row_count + row_place
        rows = slice(rb * nb, (rb + 1) * nb)
        for b in range(steps):
            at = slice(b * BASE, (b + 1) * BASE)
            value = rows_ref[rows, at]
            if b:
                value = value - exact_dot(panel[rows, : b * BASE], work[: b * BASE, at], ((1,), (0,)))
            panel[rows, at] = exact_dot(value, inverse_ref[at, :], ((1,), (1,)))
        if rb == 0:
            for k in range(2):
                at = slice(k * nb, (k + 1) * nb)
                keep = (block_row > k) | ((block_row == k) & (row_in >= col_in))
                panel[rows, at] = jnp.where(keep, panel[rows, at], 0.0)
            left = jnp.concatenate(
                [
                    jnp.where(block_row > k, panel[rows, k * nb : (k + 1) * nb], 0.0)
                    for k in range(2)
                ],
                axis=1,
            )
        else:
            left = panel[rows, :]
        product = split_dot(halves(left), solved, ((1,), (0,)))
        out_ref[rows, :] = own_ref[rows, :] - product[:, :width]
        rhs_now = own_rhs_ref[rows, :] - product[:, width:]
        if rb == 0:
            for k in range(2):
                rhs_now = jnp.where(block_row == k, cols[k * nb : (k + 1) * nb, width:], rhs_now)
        out_rhs_ref[rows, :] = rhs_now
        for k in range(2):

            @pl.when(col_place == k)
            def _():
                out_ref[rows, :nb] = panel[rows, k * nb : (k + 1) * nb]


def compute(nb, corner, cols, rhs, rows, own, own_rhs):
    size = corner.shape[0]
    vmem = pl.BlockSpec(memory_space=pltpu.VMEM)
    return pl.pallas_call(
        functools.partial(compute_kernel, nb),
        out_shape=(
            jax.ShapeDtypeStruct(own.shape, jnp.float32),
            jax.ShapeDtypeStruct(own_rhs.shape, jnp.float32),
        ),
        in_specs=[vmem] * 6,
        out_specs=(vmem, vmem),
        scratch_shapes=[
            pltpu.VMEM((size, size), jnp.float32),
            pltpu.VMEM((size, cols.shape[1] + rhs.shape[1]), jnp.float32),
            pltpu.VMEM((size, BASE), jnp.float32),
            pltpu.VMEM(rows.shape, jnp.float32),
        ],
        compiler_params=pltpu.CompilerParams(vmem_limit_bytes=48 * 1024 * 1024),
    )(corner, cols, rhs, rows, own, own_rhs)


def shards(kernel, targets):
    row_blocks, nb, col_blocks = kernel.shape[0], kernel.shape[2], kernel.shape[3]
    width = targets.shape[3]
    row_place = lax.axis_index("row")
    col_place = lax.axis_index("col")
    own = kernel.reshape(row_blocks * nb, col_blocks * nb)
    own_rhs = targets.reshape(row_blocks * nb, width)
    head = jnp.concatenate([own[:nb], own_rhs[:nb]], axis=1)
    head = jnp.concatenate([jnp.where(row_place == k, head, 0.0) for k in range(2)], axis=0)
    head = lax.psum(head, "row")
    side = own[:, :nb]
    side = jnp.concatenate([jnp.where(col_place == k, side, 0.0) for k in range(2)], axis=1)
    side = lax.psum(side, "col")
    corner = jnp.concatenate([jnp.where(row_place == k, side[:nb], 0.0) for k in range(2)], axis=0)
    corner = lax.psum(corner, "row")
    out, out_rhs = compute(
        nb, corner, head[:, : col_blocks * nb], head[:, col_blocks * nb :], side, own, own_rhs
    )
    return out.reshape(kernel.shape), out_rhs.reshape(targets.shape)


def solution(mesh):
    return jax.shard_map(
        shards,
        mesh=mesh,
        in_specs=(P(None, "row", None, None, "col", None), P(None, "row", None, "col")),
        out_specs=(P(None, "row", None, None, "col", None), P(None, "row", None, "col")),
        check_vma=False,
    )
```

```python
import functools

import jax
import jax.numpy as jnp
from jax import lax
from jax.experimental import pallas as pl
from jax.experimental.pallas import tpu as pltpu
from jax.sharding import PartitionSpec as P

STEP = 8
BASE = 128


def exact_dot(a, b, dims):
    return lax.dot_general(
        a, b, (dims, ((), ())), precision=lax.Precision.HIGHEST, preferred_element_type=jnp.float32
    )


def halves(a):
    high = a.astype(jnp.bfloat16)
    low = (a - high.astype(jnp.float32)).astype(jnp.bfloat16)
    return high, low


def split_dot(a, b, dims):
    def dot(x, y):
        return lax.dot_general(x, y, (dims, ((), ())), preferred_element_type=jnp.float32)

    a_high, a_low = a
    b_high, b_low = b
    return dot(a_high, b_high) + (dot(a_high, b_low) + dot(a_low, b_high))


def base_inverse(block):
    groups = BASE // STEP
    rows = lax.broadcasted_iota(jnp.int32, (STEP, BASE), 0)
    lanes = lax.broadcasted_iota(jnp.int32, (STEP, BASE), 1)
    full = (STEP, BASE)
    main = [block[STEP * p : STEP * (p + 1), :] for p in range(groups)]
    side = [(lanes == rows + STEP * p).astype(jnp.float32) for p in range(groups)]
    done = []
    for q in range(groups):
        here = main[q]
        first = STEP * q
        columns = [jnp.broadcast_to(here[:, first + j : first + j + 1], full) for j in range(STEP)]
        spot = [
            [jnp.broadcast_to(columns[j][i : i + 1, :], full) if i <= j else None for j in range(STEP)]
            for i in range(STEP)
        ]
        mains = [jnp.broadcast_to(here[i : i + 1, :], full) for i in range(STEP)]
        sides = [jnp.broadcast_to(side[q][i : i + 1, :], full) for i in range(STEP)]
        ratio = [[None] * STEP for _ in range(STEP)]
        recips = []
        for k in range(STEP):
            recip = 1.0 / spot[k][k]
            recips.append(recip)
            for i in range(k + 1, STEP):
                ratio[k][i] = spot[k][i] * recip
            for i in range(k + 1, STEP):
                for j in range(i, STEP):
                    spot[i][j] = spot[i][j] - ratio[k][i] * spot[k][j]
                mains[i] = mains[i] - ratio[k][i] * mains[k]
                sides[i] = sides[i] - ratio[k][i] * sides[k]
        scaled = jnp.zeros(full, jnp.float32)
        for k in range(STEP):
            scaled = jnp.where(rows == k, sides[k] * lax.rsqrt(spot[k][k]), scaled)
        done.append(scaled)
        if q == groups - 1:
            break
        mains = [mains[k] * recips[k] for k in range(STEP)]
        sides = [sides[k] * recips[k] for k in range(STEP)]
        for k in range(STEP - 1, 0, -1):
            for i in range(k):
                mains[i] = mains[i] - ratio[i][k] * mains[k]
                sides[i] = sides[i] - ratio[i][k] * sides[k]
        for p in range(q + 1, groups):
            factor = [
                jnp.broadcast_to(main[p][:, first + k : first + k + 1], full) for k in range(STEP)
            ]
            for target, source in ((main, mains), (side, sides)):
                terms = [factor[k] * source[k] for k in range(STEP)]
                while len(terms) > 1:
                    terms = [terms[t] + terms[t + 1] for t in range(0, len(terms), 2)]
                target[p] = target[p] - terms[0]
    return jnp.concatenate(done, axis=0)


MESH = pl.DeviceIdType.MESH
LANES = 128


def spread_kernel(
    nb, flat_ref, rhs_ref, rows_ref, corner_ref, head_ref,
    send_a, recv_a, send_b, recv_b, head_sems, corner_sems,
):
    height, width = rows_ref.shape
    stride = flat_ref.shape[0] // height
    row_count, col_count = lax.axis_size("row"), lax.axis_size("col")
    row_place, col_place = lax.axis_index("row"), lax.axis_index("col")
    row_odd, col_odd = lax.rem(row_place, 2), lax.rem(col_place, 2)
    next_col = (row_place, lax.rem(col_place + 2, col_count))
    past_col = (row_place, lax.rem(col_place + col_count - 2, col_count))
    pair_col = (row_place, col_place + 1 - 2 * col_odd)
    next_row = (lax.rem(row_place + 2, row_count), col_place)
    past_row = (lax.rem(row_place + row_count - 2, row_count), col_place)
    pair_row = (row_place + 1 - 2 * row_odd, col_place)

    barrier = pltpu.get_barrier_semaphore()
    friends = (next_col, past_col, pair_col, next_row, past_row, pair_row)
    for friend in friends:
        pl.semaphore_signal(barrier, inc=1, device_id=friend, device_id_type=MESH)

    for k in range(2):

        @pl.when(col_place == k)
        def _():
            for m in range(nb // LANES):
                at = slice(k * nb + m * LANES, k * nb + (m + 1) * LANES)
                rows_ref[:, at] = flat_ref[pl.ds(m, height, stride=stride), :]

        @pl.when(row_place == k)
        def _():
            here = slice(k * nb, (k + 1) * nb)
            for m in range(stride):
                at = slice(m * LANES, (m + 1) * LANES)
                head_ref[here, at] = flat_ref[pl.ds(m, nb, stride=stride), :]
            head_ref[here, stride * LANES :] = jnp.zeros(
                (nb, head_ref.shape[1] - stride * LANES), jnp.float32
            )
            head_ref[here, stride * LANES : stride * LANES + rhs_ref.shape[1]] = rhs_ref[:nb, :]

    pl.semaphore_wait(barrier, len(friends))

    def pass_on(ref, sems, index, place, count, onward, partner):
        first, second, third, fourth = sems
        chain = pltpu.make_async_remote_copy(
            src_ref=ref, dst_ref=ref, send_sem=first.at[index], recv_sem=second.at[index],
            device_id=onward, device_id_type=MESH,
        )
        pair = pltpu.make_async_remote_copy(
            src_ref=ref, dst_ref=ref, send_sem=third.at[index], recv_sem=fourth.at[index],
            device_id=partner, device_id_type=MESH,
        )

        @pl.when(place >= 2)
        def _():
            chain.wait_recv()

        @pl.when(place + 2 < count)
        def _():
            chain.start()

        pair.start()

    def finish(ref, other, sems, index, place, count, onward, partner, received):
        first, second, third, fourth = sems
        chain = pltpu.make_async_remote_copy(
            src_ref=ref, dst_ref=ref, send_sem=first.at[index], recv_sem=second.at[index],
            device_id=onward, device_id_type=MESH,
        )
        pair = pltpu.make_async_remote_copy(
            src_ref=ref, dst_ref=other, send_sem=third.at[index], recv_sem=fourth.at[index],
            device_id=partner, device_id_type=MESH,
        )

        @pl.when(place + 2 < count)
        def _():
            chain.wait_send()

        pair.wait_send()
        if not received:
            pair.wait_recv()

    half = nb // 2
    chunks = height // half
    col_sems = (send_a, recv_a, send_b, recv_b)
    mine = pl.ds(pl.multiple_of(col_odd * nb, nb), nb)
    theirs = pl.ds(pl.multiple_of((1 - col_odd) * nb, nb), nb)
    row_mine = pl.ds(pl.multiple_of(row_odd * nb, nb), nb)
    row_theirs = pl.ds(pl.multiple_of((1 - row_odd) * nb, nb), nb)
    by_col = (col_place, col_count, next_col, pair_col)
    by_row = (row_place, row_count, next_row, pair_row)

    def part(m, columns):
        return rows_ref.at[pl.ds(m * half, half), columns]

    for m in range(2):
        pass_on(part(m, mine), col_sems, m, *by_col)
    head_group = tuple(head_sems.at[j] for j in range(4))
    corner_group = tuple(corner_sems.at[j] for j in range(4))
    for m in range(2):
        pltpu.make_async_remote_copy(
            src_ref=part(m, mine), dst_ref=part(m, theirs), send_sem=send_b.at[m],
            recv_sem=recv_b.at[m], device_id=pair_col, device_id_type=MESH,
        ).wait_recv()

    @pl.when(row_place < 2)
    def _():
        corner_ref[row_mine, :] = rows_ref[:nb, :]

    pass_on(corner_ref.at[row_mine, :], corner_group, 0, *by_row)
    pass_on(part(2, mine), col_sems, 2, *by_col)
    pass_on(head_ref.at[row_mine, :], head_group, 0, *by_row)
    for m in range(3, chunks):
        pass_on(part(m, mine), col_sems, m, *by_col)
    finish(corner_ref.at[row_mine, :], corner_ref.at[row_theirs, :], corner_group, 0, *by_row, False)
    finish(head_ref.at[row_mine, :], head_ref.at[row_theirs, :], head_group, 0, *by_row, False)
    for m in range(chunks):
        finish(part(m, mine), part(m, theirs), col_sems, m, *by_col, m < 2)


def spread(nb, flat, rhs, height, width):
    vmem = pl.BlockSpec(memory_space=pltpu.VMEM)
    room = width + -(-rhs.shape[1] // LANES) * LANES
    chunks = height // (nb // 2)
    dma = pltpu.SemaphoreType.DMA
    return pl.pallas_call(
        functools.partial(spread_kernel, nb),
        out_shape=(
            jax.ShapeDtypeStruct((height, 2 * nb), jnp.float32),
            jax.ShapeDtypeStruct((2 * nb, 2 * nb), jnp.float32),
            jax.ShapeDtypeStruct((2 * nb, room), jnp.float32),
        ),
        in_specs=[vmem] * 2,
        out_specs=(vmem,) * 3,
        scratch_shapes=[dma((chunks,))] * 4 + [dma((4, 1))] * 2,
        compiler_params=pltpu.CompilerParams(
            vmem_limit_bytes=40 * 1024 * 1024, collective_id=0, has_side_effects=True
        ),
    )(flat, rhs)


def compute_kernel(
    nb, corner_ref, head_ref, rows_ref, own_ref, own_rhs_ref, out_ref, out_rhs_ref,
    work, cols, inverse_ref, panel,
):
    size = corner_ref.shape[0]
    steps = size // BASE
    stride = own_ref.shape[0] // rows_ref.shape[0]
    width = stride * LANES
    rhs_width = own_rhs_ref.shape[1]
    row_blocks = rows_ref.shape[0] // nb
    row_count = lax.axis_size("row")
    row_place = lax.axis_index("row")
    col_place = lax.axis_index("col")
    work[...] = corner_ref[...]
    cols[...] = head_ref[...]
    for b in range(steps):
        at = slice(b * BASE, (b + 1) * BASE)
        inverse = base_inverse(work[at, at])
        inverse_ref[at, :] = inverse
        cols[at, :] = exact_dot(inverse, cols[at, :], ((1,), (0,)))
        if b == steps - 1:
            break
        rest = slice((b + 1) * BASE, size)
        upper = exact_dot(inverse, work[at, rest], ((1,), (0,)))
        work[at, rest] = upper
        work[rest, rest] = work[rest, rest] - exact_dot(upper, upper, ((0,), (0,)))
        cols[rest, :] = cols[rest, :] - exact_dot(upper, cols[at, :], ((0,), (0,)))
    solved = halves(cols[...])
    row_in = lax.broadcasted_iota(jnp.int32, (nb, nb), 0)
    col_in = lax.broadcasted_iota(jnp.int32, (nb, nb), 1)
    for rb in range(row_blocks):
        block_row = rb * row_count + row_place
        rows = slice(rb * nb, (rb + 1) * nb)
        for b in range(steps):
            at = slice(b * BASE, (b + 1) * BASE)
            value = rows_ref[rows, at]
            if b:
                value = value - exact_dot(panel[rows, : b * BASE], work[: b * BASE, at], ((1,), (0,)))
            panel[rows, at] = exact_dot(value, inverse_ref[at, :], ((1,), (1,)))
        if rb == 0:
            for k in range(2):
                at = slice(k * nb, (k + 1) * nb)
                keep = (block_row > k) | ((block_row == k) & (row_in >= col_in))
                panel[rows, at] = jnp.where(keep, panel[rows, at], 0.0)
            left = jnp.concatenate(
                [
                    jnp.where(block_row > k, panel[rows, k * nb : (k + 1) * nb], 0.0)
                    for k in range(2)
                ],
                axis=1,
            )
        else:
            left = panel[rows, :]
        product = split_dot(halves(left), solved, ((1,), (0,)))
        for m in range(stride):
            spot = pl.ds(rb * nb * stride + m, nb, stride=stride)
            out_ref[spot, :] = own_ref[spot, :] - product[:, m * LANES : (m + 1) * LANES]
        rhs_now = own_rhs_ref[rows, :] - product[:, width : width + rhs_width]
        if rb == 0:
            for k in range(2):
                rhs_now = jnp.where(block_row == k, cols[k * nb : (k + 1) * nb, width : width + rhs_width], rhs_now)
        out_rhs_ref[rows, :] = rhs_now
        for k in range(2):

            @pl.when(col_place == k)
            def _():
                for m in range(nb // LANES):
                    spot = pl.ds(rb * nb * stride + m, nb, stride=stride)
                    at = slice(k * nb + m * LANES, k * nb + (m + 1) * LANES)
                    out_ref[spot, :] = panel[rows, at]


def compute(nb, corner, head, rows, own, own_rhs):
    size = corner.shape[0]
    vmem = pl.BlockSpec(memory_space=pltpu.VMEM)
    return pl.pallas_call(
        functools.partial(compute_kernel, nb),
        out_shape=(
            jax.ShapeDtypeStruct(own.shape, jnp.float32),
            jax.ShapeDtypeStruct(own_rhs.shape, jnp.float32),
        ),
        in_specs=[vmem] * 5,
        out_specs=(vmem, vmem),
        scratch_shapes=[
            pltpu.VMEM((size, size), jnp.float32),
            pltpu.VMEM(head.shape, jnp.float32),
            pltpu.VMEM((size, BASE), jnp.float32),
            pltpu.VMEM(rows.shape, jnp.float32),
        ],
        compiler_params=pltpu.CompilerParams(vmem_limit_bytes=48 * 1024 * 1024),
    )(corner, head, rows, own, own_rhs)


def shards(kernel, targets):
    row_blocks, nb, col_blocks = kernel.shape[0], kernel.shape[2], kernel.shape[3]
    width = targets.shape[3]
    height, breadth = row_blocks * nb, col_blocks * nb
    own = kernel.reshape(height * breadth // LANES, LANES)
    own_rhs = targets.reshape(height, width)
    rows, corner, head = spread(nb, own, own_rhs, height, breadth)
    out, out_rhs = compute(nb, corner, head, rows, own, own_rhs)
    return out.reshape(kernel.shape), out_rhs.reshape(targets.shape)


def solution(mesh):
    return jax.shard_map(
        shards,
        mesh=mesh,
        in_specs=(P(None, "row", None, None, "col", None), P(None, "row", None, "col")),
        out_specs=(P(None, "row", None, None, "col", None), P(None, "row", None, "col")),
        check_vma=False,
    )
```

```python
import functools

import jax
import jax.numpy as jnp
from jax import lax
from jax.experimental import pallas as pl
from jax.experimental.pallas import tpu as pltpu
from jax.sharding import PartitionSpec as P

STEP = 8
BASE = 128


def exact_dot(a, b, dims):
    return lax.dot_general(
        a, b, (dims, ((), ())), precision=lax.Precision.HIGHEST, preferred_element_type=jnp.float32
    )


def halves(a):
    high = a.astype(jnp.bfloat16)
    low = (a - high.astype(jnp.float32)).astype(jnp.bfloat16)
    return high, low


def split_dot(a, b, dims):
    def dot(x, y):
        return lax.dot_general(x, y, (dims, ((), ())), preferred_element_type=jnp.float32)

    a_high, a_low = a
    b_high, b_low = b
    return dot(a_high, b_high) + (dot(a_high, b_low) + dot(a_low, b_high))


def base_inverse(block, between):
    groups = BASE // STEP
    rows = lax.broadcasted_iota(jnp.int32, (STEP, BASE), 0)
    lanes = lax.broadcasted_iota(jnp.int32, (STEP, BASE), 1)
    full = (STEP, BASE)
    main = [block[STEP * p : STEP * (p + 1), :] for p in range(groups)]
    side = [(lanes == rows + STEP * p).astype(jnp.float32) for p in range(groups)]
    done = []
    for q in range(groups):
        here = main[q]
        first = STEP * q
        columns = [jnp.broadcast_to(here[:, first + j : first + j + 1], full) for j in range(STEP)]
        spot = [
            [jnp.broadcast_to(columns[j][i : i + 1, :], full) if i <= j else None for j in range(STEP)]
            for i in range(STEP)
        ]
        mains = [jnp.broadcast_to(here[i : i + 1, :], full) for i in range(STEP)]
        sides = [jnp.broadcast_to(side[q][i : i + 1, :], full) for i in range(STEP)]
        ratio = [[None] * STEP for _ in range(STEP)]
        recips = []
        for k in range(STEP):
            recip = 1.0 / spot[k][k]
            recips.append(recip)
            for i in range(k + 1, STEP):
                ratio[k][i] = spot[k][i] * recip
            for i in range(k + 1, STEP):
                for j in range(i, STEP):
                    spot[i][j] = spot[i][j] - ratio[k][i] * spot[k][j]
                mains[i] = mains[i] - ratio[k][i] * mains[k]
                sides[i] = sides[i] - ratio[k][i] * sides[k]
        scaled = jnp.zeros(full, jnp.float32)
        for k in range(STEP):
            scaled = jnp.where(rows == k, sides[k] * lax.rsqrt(spot[k][k]), scaled)
        done.append(scaled)
        if q % 4 == 3:
            between()
        if q == groups - 1:
            break
        mains = [mains[k] * recips[k] for k in range(STEP)]
        sides = [sides[k] * recips[k] for k in range(STEP)]
        for k in range(STEP - 1, 0, -1):
            for i in range(k):
                mains[i] = mains[i] - ratio[i][k] * mains[k]
                sides[i] = sides[i] - ratio[i][k] * sides[k]
        for p in range(q + 1, groups):
            factor = [
                jnp.broadcast_to(main[p][:, first + k : first + k + 1], full) for k in range(STEP)
            ]
            for target, source in ((main, mains), (side, sides)):
                terms = [factor[k] * source[k] for k in range(STEP)]
                while len(terms) > 1:
                    terms = [terms[t] + terms[t + 1] for t in range(0, len(terms), 2)]
                target[p] = target[p] - terms[0]
    return jnp.concatenate(done, axis=0)


MESH = pl.DeviceIdType.MESH
LANES = 128


def fused_kernel(
    nb, flat_ref, rhs_ref, out_ref, out_rhs_ref,
    rows_ref, corner_ref, head_ref, work, cols, inverse_ref, panel,
    send_a, recv_a, send_b, recv_b, head_sems, corner_sems,
):
    height, width = rows_ref.shape
    stride = flat_ref.shape[0] // height
    row_count, col_count = lax.axis_size("row"), lax.axis_size("col")
    row_place, col_place = lax.axis_index("row"), lax.axis_index("col")
    row_odd, col_odd = lax.rem(row_place, 2), lax.rem(col_place, 2)
    next_col = (row_place, lax.rem(col_place + 2, col_count))
    past_col = (row_place, lax.rem(col_place + col_count - 2, col_count))
    pair_col = (row_place, col_place + 1 - 2 * col_odd)
    next_row = (lax.rem(row_place + 2, row_count), col_place)
    past_row = (lax.rem(row_place + row_count - 2, row_count), col_place)
    pair_row = (row_place + 1 - 2 * row_odd, col_place)

    barrier = pltpu.get_barrier_semaphore()
    friends = (next_col, past_col, pair_col, next_row, past_row, pair_row)
    for friend in friends:
        pl.semaphore_signal(barrier, inc=1, device_id=friend, device_id_type=MESH)

    for k in range(2):

        @pl.when(col_place == k)
        def _():
            for m in range(nb // LANES):
                at = slice(k * nb + m * LANES, k * nb + (m + 1) * LANES)
                rows_ref[:, at] = flat_ref[pl.ds(m, height, stride=stride), :]

        @pl.when(row_place == k)
        def _():
            here = slice(k * nb, (k + 1) * nb)
            for m in range(stride):
                at = slice(m * LANES, (m + 1) * LANES)
                head_ref[here, at] = flat_ref[pl.ds(m, nb, stride=stride), :]
            head_ref[here, stride * LANES :] = jnp.zeros(
                (nb, head_ref.shape[1] - stride * LANES), jnp.float32
            )
            head_ref[here, stride * LANES : stride * LANES + rhs_ref.shape[1]] = rhs_ref[:nb, :]

    pl.semaphore_wait(barrier, len(friends))

    def pass_on(ref, sems, index, place, count, onward, partner):
        first, second, third, fourth = sems
        chain = pltpu.make_async_remote_copy(
            src_ref=ref, dst_ref=ref, send_sem=first.at[index], recv_sem=second.at[index],
            device_id=onward, device_id_type=MESH,
        )
        pair = pltpu.make_async_remote_copy(
            src_ref=ref, dst_ref=ref, send_sem=third.at[index], recv_sem=fourth.at[index],
            device_id=partner, device_id_type=MESH,
        )

        @pl.when(place >= 2)
        def _():
            chain.wait_recv()

        @pl.when(place + 2 < count)
        def _():
            chain.start()

        pair.start()

    def finish(ref, other, sems, index, place, count, onward, partner, received):
        first, second, third, fourth = sems
        chain = pltpu.make_async_remote_copy(
            src_ref=ref, dst_ref=ref, send_sem=first.at[index], recv_sem=second.at[index],
            device_id=onward, device_id_type=MESH,
        )
        pair = pltpu.make_async_remote_copy(
            src_ref=ref, dst_ref=other, send_sem=third.at[index], recv_sem=fourth.at[index],
            device_id=partner, device_id_type=MESH,
        )

        @pl.when(place + 2 < count)
        def _():
            chain.wait_send()

        pair.wait_send()
        if not received:
            pair.wait_recv()

    half = nb // 2
    chunks = height // half
    col_sems = (send_a, recv_a, send_b, recv_b)
    mine = pl.ds(pl.multiple_of(col_odd * nb, nb), nb)
    theirs = pl.ds(pl.multiple_of((1 - col_odd) * nb, nb), nb)
    row_mine = pl.ds(pl.multiple_of(row_odd * nb, nb), nb)
    row_theirs = pl.ds(pl.multiple_of((1 - row_odd) * nb, nb), nb)
    by_col = (col_place, col_count, next_col, pair_col)
    by_row = (row_place, row_count, next_row, pair_row)

    def part(m, columns):
        return rows_ref.at[pl.ds(m * half, half), columns]

    for m in range(2):
        pass_on(part(m, mine), col_sems, m, *by_col)
    head_group = tuple(head_sems.at[j] for j in range(4))
    corner_group = tuple(corner_sems.at[j] for j in range(4))
    for m in range(2):
        pltpu.make_async_remote_copy(
            src_ref=part(m, mine), dst_ref=part(m, theirs), send_sem=send_b.at[m],
            recv_sem=recv_b.at[m], device_id=pair_col, device_id_type=MESH,
        ).wait_recv()

    @pl.when(row_place < 2)
    def _():
        corner_ref[row_mine, :] = rows_ref[:nb, :]

    pass_on(corner_ref.at[row_mine, :], corner_group, 0, *by_row)
    finish(corner_ref.at[row_mine, :], corner_ref.at[row_theirs, :], corner_group, 0, *by_row, False)
    events = {}
    events[1] = lambda: pass_on(head_ref.at[row_mine, :], head_group, 0, *by_row)
    for m in range(2, chunks):
        slot = 0 if m == 2 else 2 * m - 3
        events[slot] = functools.partial(pass_on, part(m, mine), col_sems, m, *by_col)
    order = [events[slot] for slot in sorted(events)]
    slots = sorted(events)
    passed = [0, 0]

    def between():
        while passed[1] < len(order) and slots[passed[1]] <= passed[0]:
            order[passed[1]]()
            passed[1] += 1
        passed[0] += 1

    size = corner_ref.shape[0]
    steps = size // BASE
    width = stride * LANES
    rhs_width = rhs_ref.shape[1]
    row_blocks = rows_ref.shape[0] // nb
    work[...] = corner_ref[...]
    for b in range(steps):
        at = slice(b * BASE, (b + 1) * BASE)
        inverse = base_inverse(work[at, at], between)
        if b == 0:
            finish(
                head_ref.at[row_mine, :], head_ref.at[row_theirs, :], head_group, 0, *by_row, False
            )
            cols[...] = head_ref[...]
        inverse_ref[at, :] = inverse
        cols[at, :] = exact_dot(inverse, cols[at, :], ((1,), (0,)))
        if b == steps - 1:
            break
        rest = slice((b + 1) * BASE, size)
        upper = exact_dot(inverse, work[at, rest], ((1,), (0,)))
        work[at, rest] = upper
        work[rest, rest] = work[rest, rest] - exact_dot(upper, upper, ((0,), (0,)))
        cols[rest, :] = cols[rest, :] - exact_dot(upper, cols[at, :], ((0,), (0,)))
    while passed[1] < len(order):
        between()
    for m in range(chunks):
        finish(part(m, mine), part(m, theirs), col_sems, m, *by_col, m < 2)
    solved = halves(cols[...])
    row_in = lax.broadcasted_iota(jnp.int32, (nb, nb), 0)
    col_in = lax.broadcasted_iota(jnp.int32, (nb, nb), 1)
    for rb in range(row_blocks):
        block_row = rb * row_count + row_place
        rows = slice(rb * nb, (rb + 1) * nb)
        for b in range(steps):
            at = slice(b * BASE, (b + 1) * BASE)
            value = rows_ref[rows, at]
            if b:
                value = value - exact_dot(panel[rows, : b * BASE], work[: b * BASE, at], ((1,), (0,)))
            panel[rows, at] = exact_dot(value, inverse_ref[at, :], ((1,), (1,)))
        if rb == 0:
            for k in range(2):
                at = slice(k * nb, (k + 1) * nb)
                keep = (block_row > k) | ((block_row == k) & (row_in >= col_in))
                panel[rows, at] = jnp.where(keep, panel[rows, at], 0.0)
            left = jnp.concatenate(
                [
                    jnp.where(block_row > k, panel[rows, k * nb : (k + 1) * nb], 0.0)
                    for k in range(2)
                ],
                axis=1,
            )
        else:
            left = panel[rows, :]
        product = split_dot(halves(left), solved, ((1,), (0,)))
        for m in range(stride):
            spot = pl.ds(rb * nb * stride + m, nb, stride=stride)
            out_ref[spot, :] = flat_ref[spot, :] - product[:, m * LANES : (m + 1) * LANES]
        rhs_now = rhs_ref[rows, :] - product[:, width : width + rhs_width]
        if rb == 0:
            for k in range(2):
                rhs_now = jnp.where(block_row == k, cols[k * nb : (k + 1) * nb, width : width + rhs_width], rhs_now)
        out_rhs_ref[rows, :] = rhs_now
        for k in range(2):

            @pl.when(col_place == k)
            def _():
                for m in range(nb // LANES):
                    spot = pl.ds(rb * nb * stride + m, nb, stride=stride)
                    at = slice(k * nb + m * LANES, k * nb + (m + 1) * LANES)
                    out_ref[spot, :] = panel[rows, at]


def fused(nb, flat, rhs, height, width):
    vmem = pl.BlockSpec(memory_space=pltpu.VMEM)
    room = width + -(-rhs.shape[1] // LANES) * LANES
    size = 2 * nb
    chunks = height // (nb // 2)
    dma = pltpu.SemaphoreType.DMA
    return pl.pallas_call(
        functools.partial(fused_kernel, nb),
        out_shape=(
            jax.ShapeDtypeStruct(flat.shape, jnp.float32),
            jax.ShapeDtypeStruct(rhs.shape, jnp.float32),
        ),
        in_specs=[vmem] * 2,
        out_specs=(vmem, vmem),
        scratch_shapes=[
            pltpu.VMEM((height, size), jnp.float32),
            pltpu.VMEM((size, size), jnp.float32),
            pltpu.VMEM((size, room), jnp.float32),
            pltpu.VMEM((size, size), jnp.float32),
            pltpu.VMEM((size, room), jnp.float32),
            pltpu.VMEM((size, BASE), jnp.float32),
            pltpu.VMEM((height, size), jnp.float32),
            *[dma((chunks,))] * 4,
            *[dma((4, 1))] * 2,
        ],
        compiler_params=pltpu.CompilerParams(
            vmem_limit_bytes=48 * 1024 * 1024, collective_id=0, has_side_effects=True
        ),
    )(flat, rhs)


def shards(kernel, targets):
    row_blocks, nb, col_blocks = kernel.shape[0], kernel.shape[2], kernel.shape[3]
    width = targets.shape[3]
    height, breadth = row_blocks * nb, col_blocks * nb
    own = kernel.reshape(height * breadth // LANES, LANES)
    own_rhs = targets.reshape(height, width)
    out, out_rhs = fused(nb, own, own_rhs, height, breadth)
    return out.reshape(kernel.shape), out_rhs.reshape(targets.shape)


def solution(mesh):
    return jax.shard_map(
        shards,
        mesh=mesh,
        in_specs=(P(None, "row", None, None, "col", None), P(None, "row", None, "col")),
        out_specs=(P(None, "row", None, None, "col", None), P(None, "row", None, "col")),
        check_vma=False,
    )
```

```python
import functools

import jax
import jax.numpy as jnp
from jax import lax
from jax.experimental import pallas as pl
from jax.experimental.pallas import tpu as pltpu
from jax.sharding import PartitionSpec as P

STEP = 8
BASE = 128


def exact_dot(a, b, dims):
    return lax.dot_general(
        a, b, (dims, ((), ())), precision=lax.Precision.HIGHEST, preferred_element_type=jnp.float32
    )


def halves(a):
    high = a.astype(jnp.bfloat16)
    low = (a - high.astype(jnp.float32)).astype(jnp.bfloat16)
    return high, low


def split_dot(a, b, dims):
    def dot(x, y):
        return lax.dot_general(x, y, (dims, ((), ())), preferred_element_type=jnp.float32)

    a_high, a_low = a
    b_high, b_low = b
    return dot(a_high, b_high) + (dot(a_high, b_low) + dot(a_low, b_high))


def base_inverse(block, between):
    groups = BASE // STEP
    rows = lax.broadcasted_iota(jnp.int32, (STEP, BASE), 0)
    lanes = lax.broadcasted_iota(jnp.int32, (STEP, BASE), 1)
    full = (STEP, BASE)
    main = [block[STEP * p : STEP * (p + 1), :] for p in range(groups)]
    side = [(lanes == rows + STEP * p).astype(jnp.float32) for p in range(groups)]
    done = []
    for q in range(groups):
        here = main[q]
        first = STEP * q
        columns = [jnp.broadcast_to(here[:, first + j : first + j + 1], full) for j in range(STEP)]
        spot = [
            [jnp.broadcast_to(columns[j][i : i + 1, :], full) if i <= j else None for j in range(STEP)]
            for i in range(STEP)
        ]
        mains = [jnp.broadcast_to(here[i : i + 1, :], full) for i in range(STEP)]
        sides = [jnp.broadcast_to(side[q][i : i + 1, :], full) for i in range(STEP)]
        ratio = [[None] * STEP for _ in range(STEP)]
        recips = []
        for k in range(STEP):
            recip = 1.0 / spot[k][k]
            recips.append(recip)
            for i in range(k + 1, STEP):
                ratio[k][i] = spot[k][i] * recip
            for i in range(k + 1, STEP):
                for j in range(i, STEP):
                    spot[i][j] = spot[i][j] - ratio[k][i] * spot[k][j]
                mains[i] = mains[i] - ratio[k][i] * mains[k]
                sides[i] = sides[i] - ratio[k][i] * sides[k]
        scaled = jnp.zeros(full, jnp.float32)
        for k in range(STEP):
            scaled = jnp.where(rows == k, sides[k] * lax.rsqrt(spot[k][k]), scaled)
        done.append(scaled)
        if q % 4 == 3:
            between()
        if q == groups - 1:
            break
        mains = [mains[k] * recips[k] for k in range(STEP)]
        sides = [sides[k] * recips[k] for k in range(STEP)]
        for k in range(STEP - 1, 0, -1):
            for i in range(k):
                mains[i] = mains[i] - ratio[i][k] * mains[k]
                sides[i] = sides[i] - ratio[i][k] * sides[k]
        for p in range(q + 1, groups):
            factor = [
                jnp.broadcast_to(main[p][:, first + k : first + k + 1], full) for k in range(STEP)
            ]
            for target, source in ((main, mains), (side, sides)):
                terms = [factor[k] * source[k] for k in range(STEP)]
                while len(terms) > 1:
                    terms = [terms[t] + terms[t + 1] for t in range(0, len(terms), 2)]
                target[p] = target[p] - terms[0]
    return jnp.concatenate(done, axis=0)


MESH = pl.DeviceIdType.MESH
LANES = 128


def fused_kernel(
    nb, flat_ref, rhs_ref, out_ref, out_rhs_ref,
    rows_ref, corner_ref, head_ref, work, cols, inverse_ref, panel,
    send_a, recv_a, send_b, recv_b, head_sems, corner_sems,
):
    height, width = rows_ref.shape
    stride = flat_ref.shape[0] // height
    row_count, col_count = lax.axis_size("row"), lax.axis_size("col")
    row_place, col_place = lax.axis_index("row"), lax.axis_index("col")
    row_odd, col_odd = lax.rem(row_place, 2), lax.rem(col_place, 2)
    next_col = (row_place, lax.rem(col_place + 2, col_count))
    past_col = (row_place, lax.rem(col_place + col_count - 2, col_count))
    pair_col = (row_place, col_place + 1 - 2 * col_odd)
    next_row = (lax.rem(row_place + 2, row_count), col_place)
    past_row = (lax.rem(row_place + row_count - 2, row_count), col_place)
    pair_row = (row_place + 1 - 2 * row_odd, col_place)

    barrier = pltpu.get_barrier_semaphore()
    friends = (next_col, past_col, pair_col, next_row, past_row, pair_row)
    for friend in friends:
        pl.semaphore_signal(barrier, inc=1, device_id=friend, device_id_type=MESH)

    for k in range(2):

        @pl.when(col_place == k)
        def _():
            for m in range(nb // LANES):
                at = slice(k * nb + m * LANES, k * nb + (m + 1) * LANES)
                rows_ref[:, at] = flat_ref[pl.ds(m, height, stride=stride), :]

        @pl.when(row_place == k)
        def _():
            here = slice(k * nb, (k + 1) * nb)
            for m in range(stride):
                at = slice(m * LANES, (m + 1) * LANES)
                head_ref[here, at] = flat_ref[pl.ds(m, nb, stride=stride), :]
            head_ref[here, stride * LANES :] = jnp.zeros(
                (nb, head_ref.shape[1] - stride * LANES), jnp.float32
            )
            head_ref[here, stride * LANES : stride * LANES + rhs_ref.shape[1]] = rhs_ref[:nb, :]

    pl.semaphore_wait(barrier, len(friends))

    def pass_on(ref, sems, index, place, count, onward, partner):
        first, second, third, fourth = sems
        chain = pltpu.make_async_remote_copy(
            src_ref=ref, dst_ref=ref, send_sem=first.at[index], recv_sem=second.at[index],
            device_id=onward, device_id_type=MESH,
        )
        pair = pltpu.make_async_remote_copy(
            src_ref=ref, dst_ref=ref, send_sem=third.at[index], recv_sem=fourth.at[index],
            device_id=partner, device_id_type=MESH,
        )

        @pl.when(place >= 2)
        def _():
            chain.wait_recv()

        @pl.when(place + 2 < count)
        def _():
            chain.start()

        pair.start()

    def finish(ref, other, sems, index, place, count, onward, partner, received):
        first, second, third, fourth = sems
        chain = pltpu.make_async_remote_copy(
            src_ref=ref, dst_ref=ref, send_sem=first.at[index], recv_sem=second.at[index],
            device_id=onward, device_id_type=MESH,
        )
        pair = pltpu.make_async_remote_copy(
            src_ref=ref, dst_ref=other, send_sem=third.at[index], recv_sem=fourth.at[index],
            device_id=partner, device_id_type=MESH,
        )

        @pl.when(place + 2 < count)
        def _():
            chain.wait_send()

        pair.wait_send()
        if not received:
            pair.wait_recv()

    half = nb // 2
    chunks = height // half
    col_sems = (send_a, recv_a, send_b, recv_b)
    mine = pl.ds(pl.multiple_of(col_odd * nb, nb), nb)
    theirs = pl.ds(pl.multiple_of((1 - col_odd) * nb, nb), nb)
    row_mine = pl.ds(pl.multiple_of(row_odd * nb, nb), nb)
    row_theirs = pl.ds(pl.multiple_of((1 - row_odd) * nb, nb), nb)
    by_col = (col_place, col_count, next_col, pair_col)
    by_row = (row_place, row_count, next_row, pair_row)

    def part(m, columns):
        return rows_ref.at[pl.ds(m * half, half), columns]

    for m in range(2):
        pass_on(part(m, mine), col_sems, m, *by_col)
    head_group = tuple(head_sems.at[j] for j in range(4))
    corner_group = tuple(corner_sems.at[j] for j in range(4))
    def corner_half(odd, m):
        return corner_ref.at[pl.ds(pl.multiple_of(odd * nb + m * half, half), half), :]

    for m in range(2):
        pltpu.make_async_remote_copy(
            src_ref=part(m, mine), dst_ref=part(m, theirs), send_sem=send_b.at[m],
            recv_sem=recv_b.at[m], device_id=pair_col, device_id_type=MESH,
        ).wait_recv()

        @pl.when(row_place < 2)
        def _():
            corner_half(row_odd, m)[...] = part(m, slice(None))[...]

        pass_on(corner_half(row_odd, m), corner_group, m, *by_row)

    def take_corner(m):
        finish(
            corner_half(row_odd, m), corner_half(1 - row_odd, m), corner_group, m, *by_row, False
        )
        for k in range(2):
            at = slice(k * nb + m * half, k * nb + (m + 1) * half)
            work[at, :] = corner_ref[at, :]

    take_corner(0)
    events = {}
    events[1] = lambda: pass_on(head_ref.at[row_mine, :], head_group, 0, *by_row)
    for m in range(2, chunks):
        slot = 0 if m == 2 else 2 * m - 3
        events[slot] = functools.partial(pass_on, part(m, mine), col_sems, m, *by_col)
    order = [events[slot] for slot in sorted(events)]
    slots = sorted(events)
    passed = [0, 0]

    def between():
        while passed[1] < len(order) and slots[passed[1]] <= passed[0]:
            order[passed[1]]()
            passed[1] += 1
        passed[0] += 1

    size = corner_ref.shape[0]
    steps = size // BASE
    width = stride * LANES
    rhs_width = rhs_ref.shape[1]
    row_blocks = rows_ref.shape[0] // nb
    for b in range(steps):
        at = slice(b * BASE, (b + 1) * BASE)
        inverse = base_inverse(work[at, at], between)
        if b == 0:
            take_corner(1)
            finish(
                head_ref.at[row_mine, :], head_ref.at[row_theirs, :], head_group, 0, *by_row, False
            )
            cols[...] = head_ref[...]
        inverse_ref[at, :] = inverse
        cols[at, :] = exact_dot(inverse, cols[at, :], ((1,), (0,)))
        if b == steps - 1:
            break
        rest = slice((b + 1) * BASE, size)
        upper = exact_dot(inverse, work[at, rest], ((1,), (0,)))
        work[at, rest] = upper
        work[rest, rest] = work[rest, rest] - exact_dot(upper, upper, ((0,), (0,)))
        cols[rest, :] = cols[rest, :] - exact_dot(upper, cols[at, :], ((0,), (0,)))
    while passed[1] < len(order):
        between()
    for m in range(chunks):
        finish(part(m, mine), part(m, theirs), col_sems, m, *by_col, m < 2)
    solved = halves(cols[...])
    row_in = lax.broadcasted_iota(jnp.int32, (nb, nb), 0)
    col_in = lax.broadcasted_iota(jnp.int32, (nb, nb), 1)
    for rb in range(row_blocks):
        block_row = rb * row_count + row_place
        rows = slice(rb * nb, (rb + 1) * nb)
        for b in range(steps):
            at = slice(b * BASE, (b + 1) * BASE)
            value = rows_ref[rows, at]
            if b:
                value = value - exact_dot(panel[rows, : b * BASE], work[: b * BASE, at], ((1,), (0,)))
            panel[rows, at] = exact_dot(value, inverse_ref[at, :], ((1,), (1,)))
        if rb == 0:
            for k in range(2):
                at = slice(k * nb, (k + 1) * nb)
                keep = (block_row > k) | ((block_row == k) & (row_in >= col_in))
                panel[rows, at] = jnp.where(keep, panel[rows, at], 0.0)
            left = jnp.concatenate(
                [
                    jnp.where(block_row > k, panel[rows, k * nb : (k + 1) * nb], 0.0)
                    for k in range(2)
                ],
                axis=1,
            )
        else:
            left = panel[rows, :]
        product = split_dot(halves(left), solved, ((1,), (0,)))
        for m in range(stride):
            spot = pl.ds(rb * nb * stride + m, nb, stride=stride)
            out_ref[spot, :] = flat_ref[spot, :] - product[:, m * LANES : (m + 1) * LANES]
        rhs_now = rhs_ref[rows, :] - product[:, width : width + rhs_width]
        if rb == 0:
            for k in range(2):
                rhs_now = jnp.where(block_row == k, cols[k * nb : (k + 1) * nb, width : width + rhs_width], rhs_now)
        out_rhs_ref[rows, :] = rhs_now
        for k in range(2):

            @pl.when(col_place == k)
            def _():
                for m in range(nb // LANES):
                    spot = pl.ds(rb * nb * stride + m, nb, stride=stride)
                    at = slice(k * nb + m * LANES, k * nb + (m + 1) * LANES)
                    out_ref[spot, :] = panel[rows, at]


def fused(nb, flat, rhs, height, width):
    vmem = pl.BlockSpec(memory_space=pltpu.VMEM)
    room = width + -(-rhs.shape[1] // LANES) * LANES
    size = 2 * nb
    chunks = height // (nb // 2)
    dma = pltpu.SemaphoreType.DMA
    return pl.pallas_call(
        functools.partial(fused_kernel, nb),
        out_shape=(
            jax.ShapeDtypeStruct(flat.shape, jnp.float32),
            jax.ShapeDtypeStruct(rhs.shape, jnp.float32),
        ),
        in_specs=[vmem] * 2,
        out_specs=(vmem, vmem),
        scratch_shapes=[
            pltpu.VMEM((height, size), jnp.float32),
            pltpu.VMEM((size, size), jnp.float32),
            pltpu.VMEM((size, room), jnp.float32),
            pltpu.VMEM((size, size), jnp.float32),
            pltpu.VMEM((size, room), jnp.float32),
            pltpu.VMEM((size, BASE), jnp.float32),
            pltpu.VMEM((height, size), jnp.float32),
            *[dma((chunks,))] * 4,
            dma((4, 1)),
            dma((4, 2)),
        ],
        compiler_params=pltpu.CompilerParams(
            vmem_limit_bytes=48 * 1024 * 1024, collective_id=0, has_side_effects=True
        ),
    )(flat, rhs)


def shards(kernel, targets):
    row_blocks, nb, col_blocks = kernel.shape[0], kernel.shape[2], kernel.shape[3]
    width = targets.shape[3]
    height, breadth = row_blocks * nb, col_blocks * nb
    own = kernel.reshape(height * breadth // LANES, LANES)
    own_rhs = targets.reshape(height, width)
    out, out_rhs = fused(nb, own, own_rhs, height, breadth)
    return out.reshape(kernel.shape), out_rhs.reshape(targets.shape)


def solution(mesh):
    return jax.shard_map(
        shards,
        mesh=mesh,
        in_specs=(P(None, "row", None, None, "col", None), P(None, "row", None, "col")),
        out_specs=(P(None, "row", None, None, "col", None), P(None, "row", None, "col")),
        check_vma=False,
    )
```
